32 devices in a mesh: vert: 8 (over y, x, core), feat: 4 (over z).
Axes of the slice: x: 2, y: 2, z: 4, core: 2. Of those that a mesh axis runs over, the one named last changes fastest.
Arguments:
- features: bfloat16 [256, 65536], P('feat', 'vert'), may hold values from -6 to 6
- tile_vals: bfloat16 [4096, 128, 128], P('vert'), may hold values from -0.1875 to 0.1875
- tile_row: int32 [8, 512], P('vert'), may hold values from 0 to 63
- tile_col: int32 [8, 512], P('vert'), may hold values from 0 to 71
- tile_count: int32 [8], P('vert'), may hold values from 1 to 512, as said below
- recv_rows: int32 [8, 8, 128], P('vert'), may hold values from 0 to 8191
- recv_count: int32 [8, 8], P('vert'), may hold values from 0 to 128, as said below
- weight: bfloat16 [256, 256], replicated, may hold values from -0.375 to 0.375
- bias: float32 [256], replicated, may hold values from -4 to 4
Outputs:
- layer_out: bfloat16 [65536, 256], P(('vert', 'feat'))
The draws below stay inside these ranges and needn't reach their ends.
Inputs may be any that keep to these rules, and one draw needn't show every extreme that they name: `tile_count`: tile slots at or past a partition's count are padding with arbitrary contents; some partition uses all 512 slots. `recv_count`: slots at or past the count hold arbitrary valid vertices; some pair uses all 128 slots.
All inputs are finite; a program needn't handle non-finite values.
Results may differ from the reference program's by a relative error of at most 0.0075.
Values may be sent and summed in bfloat16 or wider, within the bound.
A program may use at most 256 MiB of HBM per device.

```python
import jax
import jax.numpy as jnp
from jax import lax

FIN = 256
FOUT = 256
BLOCK = 128
V_DEV = 8192
TILES = 512
SLOT = 128
NODES = 65536
NCOLB = 72
N_VERT = 8


def draw_tile_count(key, part):
    first, second = jax.random.split(jax.random.fold_in(key, 11))
    counts = jax.random.randint(first, (N_VERT,), max(1, TILES // 4), max(2, TILES // 2 + 1))
    chosen = jax.random.randint(second, (), 0, N_VERT)
    return jnp.where(jnp.arange(N_VERT) == chosen, TILES, counts).astype(jnp.int32)


def draw_recv_count(key, part):
    first, second = jax.random.split(jax.random.fold_in(key, 23))
    counts = jax.random.randint(first, (N_VERT, N_VERT), 0, SLOT + 1)
    chosen = jax.random.randint(second, (), 0, N_VERT * N_VERT)
    flat = jnp.where(jnp.arange(N_VERT * N_VERT) == chosen, SLOT, counts.reshape(-1))
    return flat.reshape(N_VERT, N_VERT).astype(jnp.int32)


def set_ends(entries, own_key, least, largest):
    longest = entries.shape.index(max(entries.shape))
    spots = []
    for shift in (0, 1):
        where = [jax.random.randint(jax.random.fold_in(own_key, axis), (), 0, length) for axis, length in enumerate(entries.shape)]
        where[longest] = (where[longest] + shift) % entries.shape[longest]
        spots.append(tuple(where))
    return entries.at[spots[0]].set(least).at[spots[1]].set(largest)


def shard_levels(rng, dims, cuts, smallest, largest):
    def one(position, blocks):
        draws = jax.random.uniform(jax.random.fold_in(jax.random.fold_in(rng, 6), position), (blocks,), jnp.float32, smallest / len(cuts), largest / len(cuts))
        return jnp.repeat(jnp.exp(draws), dims[position] // blocks).reshape((-1,) + (1,) * (len(dims) - position - 1))

    level = one(*cuts[0])
    for cut in cuts[1:]:
        level = level * one(*cut)
    return level


def gaussian(rng, extent, width, most, pieces=(), held_as=jnp.bfloat16):
    factor_of = shard_levels(rng, extent, pieces, -0.22, 0.18) if pieces else 1.0
    result = jax.random.normal(rng, extent, jnp.float32) * width * factor_of
    return jnp.minimum(jnp.maximum(result, -most), most).astype(held_as)


def setup_inputs(seed: int = 0) -> dict:
    arg_keys = jax.random.split(jax.random.key(seed), 10)
    return {
        "features": gaussian(arg_keys[0], (FIN, NODES), 1.0, 6.0, ((0, 4), (1, 8))),
        "tile_vals": gaussian(arg_keys[1], (N_VERT * TILES, BLOCK, BLOCK), (BLOCK * TILES * BLOCK // V_DEV) ** -0.5, 0.1875, ((0, 8),)),
        "tile_row": set_ends(jax.random.randint(arg_keys[2], (N_VERT, TILES), 0, V_DEV // BLOCK), jax.random.fold_in(arg_keys[2], 1), 0, (V_DEV // BLOCK) - 1).astype(jnp.int32),
        "tile_col": set_ends(jax.random.randint(arg_keys[3], (N_VERT, TILES), 0, NCOLB), jax.random.fold_in(arg_keys[3], 1), 0, NCOLB - 1).astype(jnp.int32),
        "tile_count": draw_tile_count(jax.random.fold_in(arg_keys[9], 71), 0),
        "recv_rows": set_ends(jax.random.randint(arg_keys[5], (N_VERT, N_VERT, SLOT), 0, V_DEV), jax.random.fold_in(arg_keys[5], 1), 0, V_DEV - 1).astype(jnp.int32),
        "recv_count": draw_recv_count(jax.random.fold_in(arg_keys[9], 71), 0),
        "weight": gaussian(arg_keys[7], (FIN, FOUT), FIN ** -0.5, 0.375),
        "bias": gaussian(arg_keys[8], (FOUT,), 1.0, 4.0, (), jnp.float32),
    }


def one_partition(args, flat_rows):
    local, vals, rows_blk, cols_blk, count, asked, asked_count = args
    owners = jnp.arange(N_VERT, dtype=jnp.int32)[:, None] * V_DEV
    index = (owners + asked.astype(jnp.int32)).reshape(-1)
    remote = flat_rows[index].reshape(N_VERT, SLOT, FIN)
    usable = jnp.arange(SLOT, dtype=jnp.int32)[None, :] < asked_count[:, None]
    remote = jnp.where(usable[:, :, None], remote, jnp.zeros_like(remote))
    rowbuf = jnp.concatenate([local, remote.reshape(N_VERT * SLOT, FIN)], axis=0)
    blocks = rowbuf.reshape(NCOLB, BLOCK, FIN)[cols_blk]
    product = jnp.einsum("tij,tjf->tif", vals.astype(jnp.float32), blocks.astype(jnp.float32), precision=lax.Precision.HIGHEST)
    used = (jnp.arange(TILES, dtype=jnp.int32) < count).astype(jnp.float32)
    onehot = (rows_blk[None, :] == jnp.arange(V_DEV // BLOCK, dtype=jnp.int32)[:, None]).astype(jnp.float32) * used[None, :]
    aggregate = jnp.einsum("rt,tif->rif", onehot, product, precision=lax.Precision.HIGHEST)
    return aggregate.reshape(V_DEV, FIN).astype(jnp.bfloat16)


def reference(features, tile_vals, tile_row, tile_col, tile_count, recv_rows, recv_count, weight, bias):
    flat_rows = features.T
    per_part = (flat_rows.reshape(N_VERT, V_DEV, FIN), tile_vals.reshape(N_VERT, TILES, BLOCK, BLOCK), tile_row, tile_col, tile_count, recv_rows, recv_count)
    aggregate = lax.map(lambda a: one_partition(a, flat_rows), per_part).reshape(N_VERT * V_DEV, FIN)
    hidden = jnp.dot(aggregate, weight, preferred_element_type=jnp.float32) + bias
    return jnp.maximum(hidden, 0.0).astype(jnp.bfloat16)
```

```python
import functools

import jax
import jax.numpy as jnp
from jax import lax
from jax.experimental import pallas as pl
from jax.experimental.pallas import tpu as pltpu
from jax.sharding import PartitionSpec as P

MESH = pl.DeviceIdType.MESH
PAIR = 2
GROUP = 32
BUFFERS = 3
T_BITS, C_BITS = 12, 8


def lane_block(i, size):
    return pl.ds(pl.multiple_of(i * size, size), size)


def fetch_kernel(
    parts, pieces, size, row_ref, col_ref, count_ref, rows_ref, rcount_ref, feat_hbm,
    remote, plan,
    feat, by_row, asks, wanted, wanted_s, picked, outgoing, tmp,
    fsem, qsend, qrecv, ssem, rsend, rrecv,
):
    me = lax.axis_index("vert")
    width, v_rows = feat.shape
    slots = asks.shape[1]
    load = pltpu.make_async_copy(feat_hbm, feat, fsem.at[0])
    load.start()

    bar = pltpu.get_barrier_semaphore()

    def greet(k, _):
        pl.semaphore_signal(
            bar, inc=1, device_id={"vert": lax.rem(me + k, parts)}, device_id_type=MESH
        )
        return 0

    lax.fori_loop(1, parts, greet, 0)
    lane = lax.broadcasted_iota(jnp.int32, (parts, slots), 1)
    asks[...] = jnp.where(lane < rcount_ref[...], rows_ref[0], v_rows)
    pl.semaphore_wait(bar, parts - 1)

    def ask(k, fn):
        to = lax.rem(me + k, parts)
        return pltpu.make_async_remote_copy(
            src_ref=asks.at[pl.ds(to, 1)], dst_ref=wanted.at[pl.ds(me, 1)],
            send_sem=qsend.at[to], recv_sem=qrecv.at[me],
            device_id={"vert": to}, device_id_type=MESH,
        )

    def start_ask(k, _):
        ask(k, 0).start()
        return 0

    lax.fori_loop(1, parts, start_ask, 0)
    wanted[pl.ds(me, 1), :] = asks[pl.ds(me, 1), :]

    load.wait()

    def turn(i, _):
        block = feat[:, lane_block(i, size)].astype(jnp.float32)
        by_row[lane_block(i, size), :] = block.T
        return 0

    lax.fori_loop(0, v_rows // size, turn, 0, unroll=4)
    by_row[pl.ds(v_rows, 8), :] = jnp.zeros((8, width), jnp.float32)

    def wait_ask(k, _):
        src = lax.rem(me + k, parts)
        pltpu.make_async_remote_copy(
            src_ref=asks.at[pl.ds(src, 1)], dst_ref=wanted.at[pl.ds(src, 1)],
            send_sem=qsend.at[src], recv_sem=qrecv.at[src],
            device_id={"vert": src}, device_id_type=MESH,
        ).wait()
        return 0

    lax.fori_loop(1, parts, wait_ask, 0)
    to_scalars = pltpu.make_async_copy(wanted, wanted_s, ssem.at[0])
    to_scalars.start()
    to_scalars.wait()

    def pick(p):
        def some(i, _):
            for u in range(16):
                s = i * 16 + u
                picked[pl.ds(s, 1), :] = by_row[pl.ds(wanted_s[p, s], 1), :]
            return 0

        lax.fori_loop(0, slots // 16, some, 0)
        return picked[...].T.astype(jnp.bfloat16)

    def answer(k):
        to = lax.rem(me + k, parts)
        return pltpu.make_async_remote_copy(
            src_ref=outgoing.at[to], dst_ref=remote.at[:, lane_block(me, slots)],
            send_sem=rsend.at[to], recv_sem=rrecv.at[me],
            device_id={"vert": to}, device_id_type=MESH,
        )

    def start_answer(k, _):
        to = lax.rem(me + k, parts)
        outgoing[to] = pick(to)
        answer(k).start()
        return 0

    lax.fori_loop(1, parts, start_answer, 0)
    remote[:, lane_block(me, slots)] = pick(me)

    make_plan(pieces, v_rows // size, v_rows // size + parts, row_ref, col_ref, count_ref, plan, tmp)

    def wait_answer(k, _):
        src = lax.rem(me + k, parts)
        pltpu.make_async_remote_copy(
            src_ref=outgoing.at[src], dst_ref=remote.at[:, lane_block(src, slots)],
            send_sem=rsend.at[src], recv_sem=rrecv.at[src],
            device_id={"vert": src}, device_id_type=MESH,
        ).wait()
        return 0

    lax.fori_loop(1, parts, wait_answer, 0)


def make_plan(pieces, n_rows, zero_col, row_ref, col_ref, count_ref, plan, tmp):
    n_tiles = row_ref.shape[1]
    length = plan.shape[1]
    t_lane = lax.broadcasted_iota(jnp.int32, (1, n_tiles), 1)
    used = t_lane < count_ref[0]
    row = jnp.where(used, row_ref[...], n_rows)
    r_sub = lax.broadcasted_iota(jnp.int32, (n_rows, n_tiles), 0)
    held = jnp.sum((r_sub == row).astype(jnp.int32), axis=1, keepdims=True)
    padded = (held + (PAIR - 1)) & ~(PAIR - 1)
    start = jnp.sum(jnp.where(r_sub < row, padded, 0), axis=0, keepdims=True)
    tmp[...] = jnp.broadcast_to(row, (128, n_tiles)).T
    step = 128
    rank = jnp.zeros((1, n_tiles), jnp.int32)
    for i in range(0, n_tiles, step):
        t_sub = lax.broadcasted_iota(jnp.int32, (step, n_tiles), 0) + i
        earlier = (tmp[i : i + step, :1] == row) & (t_sub < t_lane)
        rank += jnp.sum(earlier.astype(jnp.int32), axis=0, keepdims=True)
    place = jnp.where(used, start + rank, -1)
    value = t_lane | (col_ref[...] << T_BITS) | (row << (T_BITS + C_BITS)) | (1 << 29)
    tmp[...] = jnp.broadcast_to(place, (128, n_tiles)).T
    places = tmp[:, :1]
    tmp[...] = jnp.broadcast_to(value, (128, n_tiles)).T
    values = tmp[:, :1]
    for j in range(0, length, 128):
        s_lane = lax.broadcasted_iota(jnp.int32, (n_tiles, 128), 1) + j
        got = jnp.sum(jnp.where(places == s_lane, values, 0), axis=0, keepdims=True)
        some = got > 0
        plan[0:1, j : j + 128] = got & ((1 << T_BITS) - 1)
        plan[1:2, j : j + 128] = jnp.where(
            some, (got >> T_BITS) & ((1 << C_BITS) - 1), zero_col
        )
        plan[2:3, j : j + 128] = jnp.where(
            some, (got >> (T_BITS + C_BITS)) & 511, n_rows
        )
    r_col = lax.broadcasted_iota(jnp.int32, (n_rows, 128), 0)
    piece = lax.broadcasted_iota(jnp.int32, (n_rows, 128), 1) * (n_rows // pieces)
    plan[3:4, 0:128] = jnp.sum(jnp.where(r_col < piece, padded, 0), axis=0, keepdims=True)


def fetch(parts, pieces, features, tile_row, tile_col, tile_count, recv_rows, recv_count, size):
    width, v_rows = features.shape
    slots = recv_rows.shape[2]
    n_tiles = tile_row.shape[1]
    n_rows = v_rows // size
    length = n_tiles + n_rows * (PAIR - 1) + GROUP
    length = -(-length // 128) * 128
    vm = pl.BlockSpec(memory_space=pltpu.VMEM)
    dma = pltpu.SemaphoreType.DMA
    return pl.pallas_call(
        functools.partial(fetch_kernel, parts, pieces, size),
        out_shape=(
            jax.ShapeDtypeStruct((width, parts * slots), jnp.bfloat16),
            jax.ShapeDtypeStruct((8, length), jnp.int32),
        ),
        in_specs=[
            vm, vm, pl.BlockSpec(memory_space=pltpu.SMEM), vm, vm,
            pl.BlockSpec(memory_space=pl.ANY),
        ],
        out_specs=(vm, vm),
        scratch_shapes=[
            pltpu.VMEM((width, v_rows), jnp.bfloat16),
            pltpu.VMEM((v_rows + 8, width), jnp.float32),
            pltpu.VMEM((parts, slots), jnp.int32),
            pltpu.VMEM((parts, slots), jnp.int32),
            pltpu.SMEM((parts, slots), jnp.int32),
            pltpu.VMEM((slots, width), jnp.float32),
            pltpu.VMEM((parts, width, slots), jnp.bfloat16),
            pltpu.VMEM((n_tiles, 128), jnp.int32),
            dma((1,)), dma((parts,)), dma((parts,)), dma((1,)), dma((parts,)), dma((parts,)),
        ],
        compiler_params=pltpu.CompilerParams(
            collective_id=0, has_side_effects=True, vmem_limit_bytes=32 << 20
        ),
    )(tile_row, tile_col, tile_count, recv_rows, recv_count.reshape(parts, 1), features)


def piece_kernel(shift, pieces, plan, feat_hbm, remote_hbm, tiles, out, buf, rows, acc, sem, fsem):
    piece = lax.rem(lax.axis_index("feat") + shift, pieces)
    size = buf.shape[2]
    v_rows = feat_hbm.shape[1]
    r_rows = remote_hbm.shape[1]
    blocks = acc.shape[0] - 1
    first_row = piece * blocks
    first, last = plan[3, piece], plan[3, piece + 1]
    steps = (last - first + GROUP - 1) // GROUP

    load = pltpu.make_async_copy(feat_hbm, rows.at[:, pl.ds(0, v_rows)], fsem.at[0])
    load.start()
    load_remote = pltpu.make_async_copy(remote_hbm, rows.at[:, pl.ds(v_rows, r_rows)], fsem.at[1])
    load_remote.start()

    def issue(g):
        slot = lax.rem(g, BUFFERS)
        for u in range(GROUP):
            pltpu.make_async_copy(
                tiles.at[plan[0, first + g * GROUP + u]], buf.at[slot, u], sem.at[slot]
            ).start()

    for g in range(BUFFERS - 1):
        @pl.when(g < steps)
        def _():
            issue(g)

    rows[:, v_rows + r_rows :] = jnp.zeros((rows.shape[0], size), rows.dtype)
    acc[...] = jnp.zeros_like(acc)
    load.wait()
    load_remote.wait()

    def step(g, _):
        slot = lax.rem(g, BUFFERS)

        @pl.when(g + BUFFERS - 1 < steps)
        def _():
            issue(g + BUFFERS - 1)

        pltpu.make_async_copy(tiles.at[pl.ds(0, GROUP)], buf.at[slot], sem.at[slot]).wait()
        base = first + g * GROUP
        products = []
        for u in range(0, GROUP, PAIR):
            left = jnp.concatenate(
                [rows[:, lane_block(plan[1, base + u + k], size)] for k in range(PAIR)], axis=1
            )
            right = jnp.concatenate([buf[slot, u + k] for k in range(PAIR)], axis=1)
            products.append(
                lax.dot_general(
                    left, right, (((1,), (1,)), ((), ())), preferred_element_type=jnp.float32
                )
            )
        for u in range(0, GROUP, PAIR):
            r = plan[2, base + u] - first_row
            r = jnp.where((r < 0) | (r > blocks), blocks, r)
            acc[r] += products[u // PAIR]
        return 0

    lax.fori_loop(0, steps, step, 0)
    for i in range(blocks):
        out[:, i * size : (i + 1) * size] = acc[i].astype(out.dtype)


def one_piece(shift, pieces, plan, features, remote, tile_vals):
    width, v_rows = features.shape
    size = tile_vals.shape[1]
    own = v_rows // pieces
    whole = pl.BlockSpec(memory_space=pl.ANY)
    work = width * own * v_rows // 4
    return pl.pallas_call(
        functools.partial(piece_kernel, shift, pieces),
        out_shape=jax.ShapeDtypeStruct((width, own), jnp.bfloat16),
        in_specs=[pl.BlockSpec(memory_space=pltpu.SMEM), whole, whole, whole],
        out_specs=pl.BlockSpec(memory_space=pltpu.VMEM),
        scratch_shapes=[
            pltpu.VMEM((BUFFERS, GROUP, size, size), jnp.bfloat16),
            pltpu.VMEM((width, v_rows + remote.shape[1] + size), jnp.bfloat16),
            pltpu.VMEM((own // size + 1, width, size), jnp.float32),
            pltpu.SemaphoreType.DMA((BUFFERS,)),
            pltpu.SemaphoreType.DMA((2,)),
        ],
        compiler_params=pltpu.CompilerParams(vmem_limit_bytes=24 << 20),
        cost_estimate=pl.CostEstimate(
            flops=work, bytes_accessed=tile_vals.size * 2 // pieces, transcendentals=0
        ),
    )(plan, features, remote, tile_vals)


def project_kernel(shifts, *refs):
    pieces = len(shifts)
    parts, (w, b, out) = refs[:pieces], refs[pieces:]
    z = lax.axis_index("feat")
    width = parts[0].shape[0]
    left = jnp.concatenate([part[...] for part in parts], axis=0)
    right = jnp.concatenate(
        [w[pl.ds(pl.multiple_of(lax.rem(z - s + pieces, pieces) * width, width), width), :] for s in shifts],
        axis=0,
    )
    hidden = lax.dot_general(
        left, right, (((0,), (0,)), ((), ())), preferred_element_type=jnp.float32
    )
    out[...] = jnp.maximum(hidden + b[...], 0.0).astype(out.dtype)


def project(shifts, parts, weight, bias):
    width, own = parts[0].shape
    f_out = weight.shape[1]
    cut = 512
    return pl.pallas_call(
        functools.partial(project_kernel, shifts),
        grid=(own // cut,),
        out_shape=jax.ShapeDtypeStruct((own, f_out), jnp.bfloat16),
        in_specs=[pl.BlockSpec((width, cut), lambda i: (0, i))] * len(parts)
        + [
            pl.BlockSpec(weight.shape, lambda i: (0, 0)),
            pl.BlockSpec((1, f_out), lambda i: (0, 0)),
        ],
        out_specs=pl.BlockSpec((cut, f_out), lambda i: (i, 0)),
    )(*parts, weight, bias.reshape(1, f_out))


def on_device(
    features, tile_vals, tile_row, tile_col, tile_count, recv_rows, recv_count, weight, bias
):
    parts = lax.axis_size("vert")
    pieces = lax.axis_size("feat")
    size = tile_vals.shape[1]
    remote, plan = fetch(
        parts, pieces, features, tile_row, tile_col, tile_count, recv_rows, recv_count, size
    )
    shifts = sorted(range(1, pieces), key=lambda s: -min(s, pieces - s)) + [0]
    got = []
    for s in shifts:
        piece = one_piece(s, pieces, plan, features, remote, tile_vals)
        if s:
            piece = lax.ppermute(piece, "feat", [(i, (i + s) % pieces) for i in range(pieces)])
        got.append(piece)
    return project(shifts, got, weight, bias)


def solution(mesh):
    in_specs = (
        P("feat", "vert"),
        P("vert", None, None),
        P("vert", None),
        P("vert", None),
        P("vert"),
        P("vert", None, None),
        P("vert", None),
        P(),
        P(),
    )
    out_specs = P(("vert", "feat"), None)
    return jax.shard_map(
        on_device, mesh=mesh, in_specs=in_specs, out_specs=out_specs, check_vma=False
    )
```

```python
import functools

import jax
import jax.numpy as jnp
from jax import lax
from jax.experimental import pallas as pl
from jax.experimental.pallas import tpu as pltpu
from jax.sharding import PartitionSpec as P

MESH = pl.DeviceIdType.MESH
PAIR = 2
GROUP = 32
BUFFERS = 3
T_BITS, C_BITS = 12, 8
VMEM = 63 << 20


def lane_block(i, size):
    return pl.ds(pl.multiple_of(i * size, size), size)


def fetch_kernel(
    parts, pieces, size, row_ref, col_ref, count_ref, rows_ref, rcount_ref, feat_hbm,
    remote, plan,
    feat, by_row, asks, wanted, wanted_s, picked, outgoing, tmp,
    fsem, qsend, qrecv, ssem, rsend, rrecv,
):
    me = lax.axis_index("vert")
    width, v_rows = feat.shape
    slots = asks.shape[1]
    load = pltpu.make_async_copy(feat_hbm, feat, fsem.at[0])
    load.start()

    bar = pltpu.get_barrier_semaphore()

    def greet(k, _):
        pl.semaphore_signal(
            bar, inc=1, device_id={"vert": lax.rem(me + k, parts)}, device_id_type=MESH
        )
        return 0

    lax.fori_loop(1, parts, greet, 0)
    lane = lax.broadcasted_iota(jnp.int32, (1, slots), 1)
    for q in range(parts):
        asks[q : q + 1, :] = jnp.where(lane < rcount_ref[0, q], rows_ref[0, q : q + 1], v_rows)
    pl.semaphore_wait(bar, parts - 1)

    def ask(k, fn):
        to = lax.rem(me + k, parts)
        return pltpu.make_async_remote_copy(
            src_ref=asks.at[pl.ds(to, 1)], dst_ref=wanted.at[pl.ds(me, 1)],
            send_sem=qsend.at[to], recv_sem=qrecv.at[me],
            device_id={"vert": to}, device_id_type=MESH,
        )

    def start_ask(k, _):
        ask(k, 0).start()
        return 0

    lax.fori_loop(1, parts, start_ask, 0)
    wanted[pl.ds(me, 1), :] = asks[pl.ds(me, 1), :]

    load.wait()

    def turn(i, _):
        block = feat[:, lane_block(i, size)].astype(jnp.float32)
        by_row[lane_block(i, size), :] = block.T
        return 0

    lax.fori_loop(0, v_rows // size, turn, 0, unroll=4)
    by_row[pl.ds(v_rows, 8), :] = jnp.zeros((8, width), jnp.float32)

    def wait_ask(k, _):
        src = lax.rem(me + k, parts)
        pltpu.make_async_remote_copy(
            src_ref=asks.at[pl.ds(src, 1)], dst_ref=wanted.at[pl.ds(src, 1)],
            send_sem=qsend.at[src], recv_sem=qrecv.at[src],
            device_id={"vert": src}, device_id_type=MESH,
        ).wait()
        return 0

    lax.fori_loop(1, parts, wait_ask, 0)
    to_scalars = pltpu.make_async_copy(wanted, wanted_s, ssem.at[0])
    to_scalars.start()
    to_scalars.wait()

    def pick(p):
        def some(i, _):
            for u in range(16):
                s = i * 16 + u
                picked[pl.ds(s, 1), :] = by_row[pl.ds(wanted_s[p, s], 1), :]
            return 0

        lax.fori_loop(0, slots // 16, some, 0)
        return picked[...].T.astype(jnp.bfloat16)

    def answer(k):
        to = lax.rem(me + k, parts)
        return pltpu.make_async_remote_copy(
            src_ref=outgoing.at[to], dst_ref=remote.at[:, lane_block(me, slots)],
            send_sem=rsend.at[to], recv_sem=rrecv.at[me],
            device_id={"vert": to}, device_id_type=MESH,
        )

    def start_answer(k, _):
        to = lax.rem(me + k, parts)
        outgoing[to] = pick(to)
        answer(k).start()
        return 0

    lax.fori_loop(1, parts, start_answer, 0)
    remote[:, lane_block(me, slots)] = pick(me)

    make_plan(pieces, v_rows // size, v_rows // size + parts, row_ref, col_ref, count_ref, plan, tmp)

    def wait_answer(k, _):
        src = lax.rem(me + k, parts)
        pltpu.make_async_remote_copy(
            src_ref=outgoing.at[src], dst_ref=remote.at[:, lane_block(src, slots)],
            send_sem=rsend.at[src], recv_sem=rrecv.at[src],
            device_id={"vert": src}, device_id_type=MESH,
        ).wait()
        return 0

    lax.fori_loop(1, parts, wait_answer, 0)


def make_plan(pieces, n_rows, zero_col, row_ref, col_ref, count_ref, plan, tmp):
    n_tiles = row_ref.shape[1]
    length = plan.shape[1]
    t_lane = lax.broadcasted_iota(jnp.int32, (1, n_tiles), 1)
    used = t_lane < count_ref[0]
    row = jnp.where(used, row_ref[...], n_rows)
    r_sub = lax.broadcasted_iota(jnp.int32, (n_rows, n_tiles), 0)
    held = jnp.sum((r_sub == row).astype(jnp.int32), axis=1, keepdims=True)
    padded = (held + (PAIR - 1)) & ~(PAIR - 1)
    start = jnp.sum(jnp.where(r_sub < row, padded, 0), axis=0, keepdims=True)
    tmp[...] = jnp.broadcast_to(row, (128, n_tiles)).T
    step = 128
    rank = jnp.zeros((1, n_tiles), jnp.int32)
    for i in range(0, n_tiles, step):
        t_sub = lax.broadcasted_iota(jnp.int32, (step, n_tiles), 0) + i
        earlier = (tmp[i : i + step, :1] == row) & (t_sub < t_lane)
        rank += jnp.sum(earlier.astype(jnp.int32), axis=0, keepdims=True)
    place = jnp.where(used, start + rank, -1)
    value = t_lane | (col_ref[...] << T_BITS) | (row << (T_BITS + C_BITS)) | (1 << 29)
    tmp[...] = jnp.broadcast_to(place, (128, n_tiles)).T
    places = tmp[:, :1]
    tmp[...] = jnp.broadcast_to(value, (128, n_tiles)).T
    values = tmp[:, :1]
    for j in range(0, length, 128):
        s_lane = lax.broadcasted_iota(jnp.int32, (n_tiles, 128), 1) + j
        got = jnp.sum(jnp.where(places == s_lane, values, 0), axis=0, keepdims=True)
        some = got > 0
        plan[0:1, j : j + 128] = got & ((1 << T_BITS) - 1)
        plan[1:2, j : j + 128] = jnp.where(
            some, (got >> T_BITS) & ((1 << C_BITS) - 1), zero_col
        )
        plan[2:3, j : j + 128] = jnp.where(
            some, (got >> (T_BITS + C_BITS)) & 511, n_rows
        )
    r_col = lax.broadcasted_iota(jnp.int32, (n_rows, 128), 0)
    piece = lax.broadcasted_iota(jnp.int32, (n_rows, 128), 1) * (n_rows // pieces)
    plan[3:4, 0:128] = jnp.sum(jnp.where(r_col < piece, padded, 0), axis=0, keepdims=True)


def fetch(parts, pieces, features, tile_row, tile_col, tile_count, recv_rows, recv_count, size):
    width, v_rows = features.shape
    slots = recv_rows.shape[2]
    n_tiles = tile_row.shape[1]
    n_rows = v_rows // size
    length = n_tiles + n_rows * (PAIR - 1) + GROUP
    length = -(-length // 128) * 128
    vm = pl.BlockSpec(memory_space=pltpu.VMEM)
    dma = pltpu.SemaphoreType.DMA
    return pl.pallas_call(
        functools.partial(fetch_kernel, parts, pieces, size),
        out_shape=(
            jax.ShapeDtypeStruct((width, parts * slots), jnp.bfloat16),
            jax.ShapeDtypeStruct((8, length), jnp.int32),
        ),
        in_specs=[
            vm, vm, pl.BlockSpec(memory_space=pltpu.SMEM), vm,
            pl.BlockSpec(memory_space=pltpu.SMEM),
            pl.BlockSpec(memory_space=pl.ANY),
        ],
        out_specs=(vm, vm),
        scratch_shapes=[
            pltpu.VMEM((width, v_rows), jnp.bfloat16),
            pltpu.VMEM((v_rows + 8, width), jnp.float32),
            pltpu.VMEM((parts, slots), jnp.int32),
            pltpu.VMEM((parts, slots), jnp.int32),
            pltpu.SMEM((parts, slots), jnp.int32),
            pltpu.VMEM((slots, width), jnp.float32),
            pltpu.VMEM((parts, width, slots), jnp.bfloat16),
            pltpu.VMEM((n_tiles, 128), jnp.int32),
            dma((1,)), dma((parts,)), dma((parts,)), dma((1,)), dma((parts,)), dma((parts,)),
        ],
        compiler_params=pltpu.CompilerParams(
            collective_id=0, has_side_effects=True, vmem_limit_bytes=VMEM
        ),
    )(tile_row, tile_col, tile_count, recv_rows, recv_count, features)


def piece_kernel(shift, pieces, plan, feat_hbm, remote_hbm, tiles, out, buf, rows, acc, sem, fsem):
    piece = lax.rem(lax.axis_index("feat") + shift, pieces)
    size = buf.shape[2]
    v_rows = feat_hbm.shape[1]
    r_rows = remote_hbm.shape[1]
    blocks = acc.shape[0] - 1
    first_row = piece * blocks
    first, last = plan[3, piece], plan[3, piece + 1]
    steps = (last - first + GROUP - 1) // GROUP

    load = pltpu.make_async_copy(feat_hbm, rows.at[:, pl.ds(0, v_rows)], fsem.at[0])
    load.start()
    load_remote = pltpu.make_async_copy(remote_hbm, rows.at[:, pl.ds(v_rows, r_rows)], fsem.at[1])
    load_remote.start()

    def issue(g):
        slot = lax.rem(g, BUFFERS)
        for u in range(GROUP):
            pltpu.make_async_copy(
                tiles.at[plan[0, first + g * GROUP + u]], buf.at[slot, u], sem.at[slot]
            ).start()

    for g in range(BUFFERS - 1):
        @pl.when(g < steps)
        def _():
            issue(g)

    rows[:, v_rows + r_rows :] = jnp.zeros((rows.shape[0], size), rows.dtype)
    acc[...] = jnp.zeros_like(acc)
    load.wait()
    load_remote.wait()

    def step(g, _):
        slot = lax.rem(g, BUFFERS)

        @pl.when(g + BUFFERS - 1 < steps)
        def _():
            issue(g + BUFFERS - 1)

        pltpu.make_async_copy(tiles.at[pl.ds(0, GROUP)], buf.at[slot], sem.at[slot]).wait()
        base = first + g * GROUP
        products = []
        for u in range(0, GROUP, PAIR):
            left = jnp.concatenate(
                [rows[:, lane_block(plan[1, base + u + k], size)] for k in range(PAIR)], axis=1
            )
            right = jnp.concatenate([buf[slot, u + k] for k in range(PAIR)], axis=1)
            products.append(
                lax.dot_general(
                    left, right, (((1,), (1,)), ((), ())), preferred_element_type=jnp.float32
                )
            )
        for u in range(0, GROUP, PAIR):
            r = plan[2, base + u] - first_row
            r = jnp.where((r < 0) | (r > blocks), blocks, r)
            acc[r] += products[u // PAIR]
        return 0

    lax.fori_loop(0, steps, step, 0)
    for i in range(blocks):
        out[:, i * size : (i + 1) * size] = acc[i].astype(out.dtype)


def one_piece(shift, pieces, plan, features, remote, tile_vals):
    width, v_rows = features.shape
    size = tile_vals.shape[1]
    own = v_rows // pieces
    whole = pl.BlockSpec(memory_space=pl.ANY)
    work = width * own * v_rows // 4
    return pl.pallas_call(
        functools.partial(piece_kernel, shift, pieces),
        out_shape=jax.ShapeDtypeStruct((width, own), jnp.bfloat16),
        in_specs=[pl.BlockSpec(memory_space=pltpu.SMEM), whole, whole, whole],
        out_specs=pl.BlockSpec(memory_space=pltpu.VMEM),
        scratch_shapes=[
            pltpu.VMEM((BUFFERS, GROUP, size, size), jnp.bfloat16),
            pltpu.VMEM((width, v_rows + remote.shape[1] + size), jnp.bfloat16),
            pltpu.VMEM((own // size + 1, width, size), jnp.float32),
            pltpu.SemaphoreType.DMA((BUFFERS,)),
            pltpu.SemaphoreType.DMA((2,)),
        ],
        compiler_params=pltpu.CompilerParams(vmem_limit_bytes=VMEM),
        cost_estimate=pl.CostEstimate(
            flops=work, bytes_accessed=tile_vals.size * 2 // pieces, transcendentals=0
        ),
    )(plan, features, remote, tile_vals)


def project_kernel(shifts, *refs):
    pieces = len(shifts)
    parts, (w, b, out) = refs[:pieces], refs[pieces:]
    z = lax.axis_index("feat")
    width = parts[0].shape[0]
    left = jnp.concatenate([part[...] for part in parts], axis=0)
    right = jnp.concatenate(
        [w[pl.ds(pl.multiple_of(lax.rem(z - s + pieces, pieces) * width, width), width), :] for s in shifts],
        axis=0,
    )
    hidden = lax.dot_general(
        left, right, (((0,), (0,)), ((), ())), preferred_element_type=jnp.float32
    )
    out[...] = jnp.maximum(hidden + b[...], 0.0).astype(out.dtype)


def project(shifts, parts, weight, bias):
    width, own = parts[0].shape
    f_out = weight.shape[1]
    cut = own // 2
    return pl.pallas_call(
        functools.partial(project_kernel, shifts),
        grid=(own // cut,),
        out_shape=jax.ShapeDtypeStruct((own, f_out), jnp.bfloat16),
        in_specs=[pl.BlockSpec((width, cut), lambda i: (0, i))] * len(parts)
        + [
            pl.BlockSpec(weight.shape, lambda i: (0, 0)),
            pl.BlockSpec((1, f_out), lambda i: (0, 0)),
        ],
        out_specs=pl.BlockSpec((cut, f_out), lambda i: (i, 0)),
        compiler_params=pltpu.CompilerParams(vmem_limit_bytes=VMEM),
    )(*parts, weight, bias.reshape(1, f_out))


def on_device(
    features, tile_vals, tile_row, tile_col, tile_count, recv_rows, recv_count, weight, bias
):
    parts = lax.axis_size("vert")
    pieces = lax.axis_size("feat")
    size = tile_vals.shape[1]
    remote, plan = fetch(
        parts, pieces, features, tile_row, tile_col, tile_count, recv_rows, recv_count, size
    )
    shifts = sorted(range(1, pieces), key=lambda s: -min(s, pieces - s)) + [0]
    got = []
    for s in shifts:
        piece = one_piece(s, pieces, plan, features, remote, tile_vals)
        if s:
            piece = lax.ppermute(piece, "feat", [(i, (i + s) % pieces) for i in range(pieces)])
        got.append(piece)
    return project(shifts, got, weight, bias)


def solution(mesh):
    in_specs = (
        P("feat", "vert"),
        P("vert", None, None),
        P("vert", None),
        P("vert", None),
        P("vert"),
        P("vert", None, None),
        P("vert", None),
        P(),
        P(),
    )
    out_specs = P(("vert", "feat"), None)
    return jax.shard_map(
        on_device, mesh=mesh, in_specs=in_specs, out_specs=out_specs, check_vma=False
    )
```

```python
import functools

import jax
import jax.numpy as jnp
from jax import lax
from jax.experimental import pallas as pl
from jax.experimental.pallas import tpu as pltpu
from jax.sharding import PartitionSpec as P

MESH = pl.DeviceIdType.MESH
PAIR = 2
GROUP = 32
BUFFERS = 3
T_BITS, C_BITS = 12, 8
VMEM = 63 << 20


def lane_block(i, size):
    return pl.ds(pl.multiple_of(i * size, size), size)


def fetch_kernel(
    parts, pieces, size, row_ref, col_ref, count_ref, rows_ref, rcount_ref, feat_hbm,
    remote, plan,
    feat, by_row, asks, wanted, wanted_s, picked, outgoing, tmp,
    fsem, qsend, qrecv, ssem, rsend, rrecv,
):
    me = lax.axis_index("vert")
    width, v_rows = feat.shape
    slots = asks.shape[1]
    load = pltpu.make_async_copy(feat_hbm, feat, fsem.at[0])
    load.start()

    bar = pltpu.get_barrier_semaphore()

    def greet(k, _):
        pl.semaphore_signal(
            bar, inc=1, device_id={"vert": lax.rem(me + k, parts)}, device_id_type=MESH
        )
        return 0

    lax.fori_loop(1, parts, greet, 0)
    lane = lax.broadcasted_iota(jnp.int32, (1, slots), 1)
    for q in range(parts):
        asks[q : q + 1, :] = jnp.where(lane < rcount_ref[0, q], rows_ref[0, q : q + 1], v_rows)
    pl.semaphore_wait(bar, parts - 1)

    def ask(k, fn):
        to = lax.rem(me + k, parts)
        return pltpu.make_async_remote_copy(
            src_ref=asks.at[pl.ds(to, 1)], dst_ref=wanted.at[pl.ds(me, 1)],
            send_sem=qsend.at[to], recv_sem=qrecv.at[me],
            device_id={"vert": to}, device_id_type=MESH,
        )

    def start_ask(k, _):
        ask(k, 0).start()
        return 0

    lax.fori_loop(1, parts, start_ask, 0)
    wanted[pl.ds(me, 1), :] = asks[pl.ds(me, 1), :]

    load.wait()

    def turn(i, _):
        by_row[lane_block(i, size), :] = feat[:, lane_block(i, size)].T.astype(jnp.float32)
        return 0

    lax.fori_loop(0, v_rows // size, turn, 0, unroll=4)
    by_row[pl.ds(v_rows, 8), :] = jnp.zeros((8, width), jnp.float32)

    def wait_ask(k, _):
        src = lax.rem(me + k, parts)
        pltpu.make_async_remote_copy(
            src_ref=asks.at[pl.ds(src, 1)], dst_ref=wanted.at[pl.ds(src, 1)],
            send_sem=qsend.at[src], recv_sem=qrecv.at[src],
            device_id={"vert": src}, device_id_type=MESH,
        ).wait()
        return 0

    lax.fori_loop(1, parts, wait_ask, 0)
    to_scalars = pltpu.make_async_copy(wanted, wanted_s, ssem.at[0])
    to_scalars.start()
    to_scalars.wait()

    def pick(p):
        def some(i, _):
            found = [by_row[pl.ds(wanted_s[p, i * 32 + u], 1), :] for u in range(32)]
            for u in range(32):
                picked[pl.ds(i * 32 + u, 1), :] = found[u]
            return 0

        lax.fori_loop(0, slots // 32, some, 0)
        return picked[...].astype(jnp.bfloat16).T

    def answer(k):
        to = lax.rem(me + k, parts)
        return pltpu.make_async_remote_copy(
            src_ref=outgoing.at[to], dst_ref=remote.at[:, lane_block(me, slots)],
            send_sem=rsend.at[to], recv_sem=rrecv.at[me],
            device_id={"vert": to}, device_id_type=MESH,
        )

    def start_answer(k, _):
        to = lax.rem(me + k, parts)
        outgoing[to] = pick(to)
        answer(k).start()
        return 0

    lax.fori_loop(1, parts, start_answer, 0)
    remote[:, lane_block(me, slots)] = pick(me)

    make_plan(pieces, v_rows // size, v_rows // size + parts, row_ref, col_ref, count_ref, plan, tmp)

    def wait_answer(k, _):
        src = lax.rem(me + k, parts)
        pltpu.make_async_remote_copy(
            src_ref=outgoing.at[src], dst_ref=remote.at[:, lane_block(src, slots)],
            send_sem=rsend.at[src], recv_sem=rrecv.at[src],
            device_id={"vert": src}, device_id_type=MESH,
        ).wait()
        return 0

    lax.fori_loop(1, parts, wait_answer, 0)


def make_plan(pieces, n_rows, zero_col, row_ref, col_ref, count_ref, plan, tmp):
    n_tiles = row_ref.shape[1]
    length = plan.shape[1]
    t_lane = lax.broadcasted_iota(jnp.int32, (1, n_tiles), 1)
    used = t_lane < count_ref[0]
    row = jnp.where(used, row_ref[...], n_rows)
    r_sub = lax.broadcasted_iota(jnp.int32, (n_rows, n_tiles), 0)
    held = jnp.sum((r_sub == row).astype(jnp.int32), axis=1, keepdims=True)
    padded = (held + (PAIR - 1)) & ~(PAIR - 1)
    start = jnp.sum(jnp.where(r_sub < row, padded, 0), axis=0, keepdims=True)
    tmp[...] = jnp.broadcast_to(row, (128, n_tiles)).T
    step = 128
    rank = jnp.zeros((1, n_tiles), jnp.int32)
    for i in range(0, n_tiles, step):
        t_sub = lax.broadcasted_iota(jnp.int32, (step, n_tiles), 0) + i
        earlier = (tmp[i : i + step, :1] == row) & (t_sub < t_lane)
        rank += jnp.sum(earlier.astype(jnp.int32), axis=0, keepdims=True)
    place = jnp.where(used, start + rank, -1)
    value = t_lane | (col_ref[...] << T_BITS) | (row << (T_BITS + C_BITS)) | (1 << 29)
    tmp[...] = jnp.broadcast_to(place, (128, n_tiles)).T
    places = tmp[:, :1]
    tmp[...] = jnp.broadcast_to(value, (128, n_tiles)).T
    values = tmp[:, :1]
    for j in range(0, length, 128):
        s_lane = lax.broadcasted_iota(jnp.int32, (n_tiles, 128), 1) + j
        got = jnp.sum(jnp.where(places == s_lane, values, 0), axis=0, keepdims=True)
        some = got > 0
        plan[0:1, j : j + 128] = got & ((1 << T_BITS) - 1)
        plan[1:2, j : j + 128] = jnp.where(
            some, (got >> T_BITS) & ((1 << C_BITS) - 1), zero_col
        )
        plan[2:3, j : j + 128] = jnp.where(
            some, (got >> (T_BITS + C_BITS)) & 511, n_rows
        )
    r_col = lax.broadcasted_iota(jnp.int32, (n_rows, 128), 0)
    piece = lax.broadcasted_iota(jnp.int32, (n_rows, 128), 1) * (n_rows // pieces)
    plan[3:4, 0:128] = jnp.sum(jnp.where(r_col < piece, padded, 0), axis=0, keepdims=True)


def fetch(parts, pieces, features, tile_row, tile_col, tile_count, recv_rows, recv_count, size):
    width, v_rows = features.shape
    slots = recv_rows.shape[2]
    n_tiles = tile_row.shape[1]
    n_rows = v_rows // size
    length = n_tiles + n_rows * (PAIR - 1) + GROUP
    length = -(-length // 128) * 128
    vm = pl.BlockSpec(memory_space=pltpu.VMEM)
    dma = pltpu.SemaphoreType.DMA
    return pl.pallas_call(
        functools.partial(fetch_kernel, parts, pieces, size),
        out_shape=(
            jax.ShapeDtypeStruct((width, parts * slots), jnp.bfloat16),
            jax.ShapeDtypeStruct((8, length), jnp.int32),
        ),
        in_specs=[
            vm, vm, pl.BlockSpec(memory_space=pltpu.SMEM), vm,
            pl.BlockSpec(memory_space=pltpu.SMEM),
            pl.BlockSpec(memory_space=pl.ANY),
        ],
        out_specs=(vm, vm),
        scratch_shapes=[
            pltpu.VMEM((width, v_rows), jnp.bfloat16),
            pltpu.VMEM((v_rows + 8, width), jnp.float32),
            pltpu.VMEM((parts, slots), jnp.int32),
            pltpu.VMEM((parts, slots), jnp.int32),
            pltpu.SMEM((parts, slots), jnp.int32),
            pltpu.VMEM((slots, width), jnp.float32),
            pltpu.VMEM((parts, width, slots), jnp.bfloat16),
            pltpu.VMEM((n_tiles, 128), jnp.int32),
            dma((1,)), dma((parts,)), dma((parts,)), dma((1,)), dma((parts,)), dma((parts,)),
        ],
        compiler_params=pltpu.CompilerParams(
            collective_id=0, has_side_effects=True, vmem_limit_bytes=VMEM
        ),
    )(tile_row, tile_col, tile_count, recv_rows, recv_count, features)


def piece_kernel(shift, pieces, plan, feat_hbm, remote_hbm, tiles, out, buf, rows, acc, sem, fsem):
    piece = lax.rem(lax.axis_index("feat") + shift, pieces)
    size = buf.shape[2]
    v_rows = feat_hbm.shape[1]
    r_rows = remote_hbm.shape[1]
    blocks = acc.shape[0] - 1
    first_row = piece * blocks
    first, last = plan[3, piece], plan[3, piece + 1]
    steps = (last - first + GROUP - 1) // GROUP

    load = pltpu.make_async_copy(feat_hbm, rows.at[:, pl.ds(0, v_rows)], fsem.at[0])
    load.start()
    load_remote = pltpu.make_async_copy(remote_hbm, rows.at[:, pl.ds(v_rows, r_rows)], fsem.at[1])
    load_remote.start()

    def issue(g):
        slot = lax.rem(g, BUFFERS)
        for u in range(GROUP):
            pltpu.make_async_copy(
                tiles.at[plan[0, first + g * GROUP + u]], buf.at[slot, u], sem.at[slot]
            ).start()

    for g in range(BUFFERS - 1):
        @pl.when(g < steps)
        def _():
            issue(g)

    rows[:, v_rows + r_rows :] = jnp.zeros((rows.shape[0], size), rows.dtype)
    acc[...] = jnp.zeros_like(acc)
    load.wait()
    load_remote.wait()

    def step(g, _):
        slot = lax.rem(g, BUFFERS)

        @pl.when(g + BUFFERS - 1 < steps)
        def _():
            issue(g + BUFFERS - 1)

        pltpu.make_async_copy(tiles.at[pl.ds(0, GROUP)], buf.at[slot], sem.at[slot]).wait()
        base = first + g * GROUP
        products = []
        for u in range(0, GROUP, PAIR):
            left = jnp.concatenate(
                [rows[:, lane_block(plan[1, base + u + k], size)] for k in range(PAIR)], axis=1
            )
            right = jnp.concatenate([buf[slot, u + k] for k in range(PAIR)], axis=1)
            products.append(
                lax.dot_general(
                    left, right, (((1,), (1,)), ((), ())), preferred_element_type=jnp.float32
                )
            )
        for u in range(0, GROUP, PAIR):
            r = plan[2, base + u] - first_row
            r = jnp.where((r < 0) | (r > blocks), blocks, r)
            acc[r] += products[u // PAIR]
        return 0

    lax.fori_loop(0, steps, step, 0)
    for i in range(blocks):
        out[:, i * size : (i + 1) * size] = acc[i].astype(out.dtype)


def one_piece(shift, pieces, plan, features, remote, tile_vals):
    width, v_rows = features.shape
    size = tile_vals.shape[1]
    own = v_rows // pieces
    whole = pl.BlockSpec(memory_space=pl.ANY)
    work = width * own * v_rows // 4
    return pl.pallas_call(
        functools.partial(piece_kernel, shift, pieces),
        out_shape=jax.ShapeDtypeStruct((width, own), jnp.bfloat16),
        in_specs=[pl.BlockSpec(memory_space=pltpu.SMEM), whole, whole, whole],
        out_specs=pl.BlockSpec(memory_space=pltpu.VMEM),
        scratch_shapes=[
            pltpu.VMEM((BUFFERS, GROUP, size, size), jnp.bfloat16),
            pltpu.VMEM((width, v_rows + remote.shape[1] + size), jnp.bfloat16),
            pltpu.VMEM((own // size + 1, width, size), jnp.float32),
            pltpu.SemaphoreType.DMA((BUFFERS,)),
            pltpu.SemaphoreType.DMA((2,)),
        ],
        compiler_params=pltpu.CompilerParams(vmem_limit_bytes=VMEM),
        cost_estimate=pl.CostEstimate(
            flops=work, bytes_accessed=tile_vals.size * 2 // pieces, transcendentals=0
        ),
    )(plan, features, remote, tile_vals)


def project_kernel(shifts, *refs):
    pieces = len(shifts)
    parts, (w, b, out) = refs[:pieces], refs[pieces:]
    z = lax.axis_index("feat")
    width = parts[0].shape[0]
    left = jnp.concatenate([part[...] for part in parts], axis=0)
    right = jnp.concatenate(
        [w[pl.ds(pl.multiple_of(lax.rem(z - s + pieces, pieces) * width, width), width), :] for s in shifts],
        axis=0,
    )
    hidden = lax.dot_general(
        left, right, (((0,), (0,)), ((), ())), preferred_element_type=jnp.float32
    )
    out[...] = jnp.maximum(hidden + b[...], 0.0).astype(out.dtype)


def project(shifts, parts, weight, bias):
    width, own = parts[0].shape
    f_out = weight.shape[1]
    cut = own
    return pl.pallas_call(
        functools.partial(project_kernel, shifts),
        grid=(own // cut,),
        out_shape=jax.ShapeDtypeStruct((own, f_out), jnp.bfloat16),
        in_specs=[pl.BlockSpec((width, cut), lambda i: (0, i))] * len(parts)
        + [
            pl.BlockSpec(weight.shape, lambda i: (0, 0)),
            pl.BlockSpec((1, f_out), lambda i: (0, 0)),
        ],
        out_specs=pl.BlockSpec((cut, f_out), lambda i: (i, 0)),
        compiler_params=pltpu.CompilerParams(vmem_limit_bytes=VMEM),
    )(*parts, weight, bias.reshape(1, f_out))


def on_device(
    features, tile_vals, tile_row, tile_col, tile_count, recv_rows, recv_count, weight, bias
):
    parts = lax.axis_size("vert")
    pieces = lax.axis_size("feat")
    size = tile_vals.shape[1]
    remote, plan = fetch(
        parts, pieces, features, tile_row, tile_col, tile_count, recv_rows, recv_count, size
    )
    shifts = sorted(range(1, pieces), key=lambda s: -min(s, pieces - s)) + [0]
    got = []
    for s in shifts:
        piece = one_piece(s, pieces, plan, features, remote, tile_vals)
        if s:
            piece = lax.ppermute(piece, "feat", [(i, (i + s) % pieces) for i in range(pieces)])
        got.append(piece)
    return project(shifts, got, weight, bias)


def solution(mesh):
    in_specs = (
        P("feat", "vert"),
        P("vert", None, None),
        P("vert", None),
        P("vert", None),
        P("vert"),
        P("vert", None, None),
        P("vert", None),
        P(),
        P(),
    )
    out_specs = P(("vert", "feat"), None)
    return jax.shard_map(
        on_device, mesh=mesh, in_specs=in_specs, out_specs=out_specs, check_vma=False
    )
```

```python
import functools

import jax
import jax.numpy as jnp
from jax import lax
from jax.experimental import pallas as pl
from jax.experimental.pallas import tpu as pltpu
from jax.sharding import PartitionSpec as P

MESH = pl.DeviceIdType.MESH
PAIR = 2
GROUP = 32
BUFFERS = 3
T_BITS, C_BITS = 12, 8
VMEM = 63 << 20


def lane_block(i, size):
    return pl.ds(pl.multiple_of(i * size, size), size)


def fetch_kernel(
    parts, pieces, size, row_ref, col_ref, count_ref, rows_ref, rcount_ref, feat_hbm,
    remote, plan,
    feat, by_row, asks, wanted, wanted_s, picked, outgoing, tmp,
    fsem, qsend, qrecv, ssem, rsend, rrecv,
):
    me = lax.axis_index("vert")
    width, v_rows = feat.shape
    slots = asks.shape[1]
    load = pltpu.make_async_copy(feat_hbm, feat, fsem.at[0])
    load.start()

    bar = pltpu.get_barrier_semaphore()

    def greet(k, _):
        pl.semaphore_signal(
            bar, inc=1, device_id={"vert": lax.rem(me + k, parts)}, device_id_type=MESH
        )
        return 0

    lax.fori_loop(1, parts, greet, 0)
    lane = lax.broadcasted_iota(jnp.int32, (1, slots), 1)
    for q in range(parts):
        asks[q : q + 1, :] = jnp.where(lane < rcount_ref[0, q], rows_ref[0, q : q + 1], v_rows)
    pl.semaphore_wait(bar, parts - 1)

    def ask(k, fn):
        to = lax.rem(me + k, parts)
        return pltpu.make_async_remote_copy(
            src_ref=asks.at[pl.ds(to, 1)], dst_ref=wanted.at[pl.ds(me, 1)],
            send_sem=qsend.at[to], recv_sem=qrecv.at[me],
            device_id={"vert": to}, device_id_type=MESH,
        )

    def start_ask(k, _):
        ask(k, 0).start()
        return 0

    lax.fori_loop(1, parts, start_ask, 0)
    wanted[pl.ds(me, 1), :] = asks[pl.ds(me, 1), :]

    load.wait()

    def turn(i, _):
        by_row[lane_block(i, size), :] = feat[:, lane_block(i, size)].T.astype(jnp.float32)
        return 0

    lax.fori_loop(0, v_rows // size, turn, 0, unroll=4)
    by_row[pl.ds(v_rows, 8), :] = jnp.zeros((8, width), jnp.float32)

    def wait_ask(k, _):
        src = lax.rem(me + k, parts)
        pltpu.make_async_remote_copy(
            src_ref=asks.at[pl.ds(src, 1)], dst_ref=wanted.at[pl.ds(src, 1)],
            send_sem=qsend.at[src], recv_sem=qrecv.at[src],
            device_id={"vert": src}, device_id_type=MESH,
        ).wait()
        return 0

    lax.fori_loop(1, parts, wait_ask, 0)
    to_scalars = pltpu.make_async_copy(wanted, wanted_s, ssem.at[0])
    to_scalars.start()
    to_scalars.wait()

    def pick(p):
        def some(i, _):
            found = [by_row[pl.ds(wanted_s[p, i * 32 + u], 1), :] for u in range(32)]
            for u in range(32):
                picked[pl.ds(i * 32 + u, 1), :] = found[u]
            return 0

        lax.fori_loop(0, slots // 32, some, 0)
        return picked[...].astype(jnp.bfloat16).T

    def answer(k):
        to = lax.rem(me + k, parts)
        return pltpu.make_async_remote_copy(
            src_ref=outgoing.at[to], dst_ref=remote.at[:, lane_block(me, slots)],
            send_sem=rsend.at[to], recv_sem=rrecv.at[me],
            device_id={"vert": to}, device_id_type=MESH,
        )

    def start_answer(k, _):
        to = lax.rem(me + k, parts)
        outgoing[to] = pick(to)
        answer(k).start()
        return 0

    lax.fori_loop(1, parts, start_answer, 0)
    remote[:, lane_block(me, slots)] = pick(me)

    make_plan(pieces, v_rows // size, v_rows // size + parts, row_ref, col_ref, count_ref, plan, tmp)

    def wait_answer(k, _):
        src = lax.rem(me + k, parts)
        pltpu.make_async_remote_copy(
            src_ref=outgoing.at[src], dst_ref=remote.at[:, lane_block(src, slots)],
            send_sem=rsend.at[src], recv_sem=rrecv.at[src],
            device_id={"vert": src}, device_id_type=MESH,
        ).wait()
        return 0

    lax.fori_loop(1, parts, wait_answer, 0)


def make_plan(pieces, n_rows, zero_col, row_ref, col_ref, count_ref, plan, tmp):
    n_tiles = row_ref.shape[1]
    length = plan.shape[1]
    t_lane = lax.broadcasted_iota(jnp.int32, (1, n_tiles), 1)
    used = t_lane < count_ref[0]
    row = jnp.where(used, row_ref[...], n_rows)
    r_sub = lax.broadcasted_iota(jnp.int32, (n_rows, n_tiles), 0)
    held = jnp.sum((r_sub == row).astype(jnp.int32), axis=1, keepdims=True)
    padded = (held + (PAIR - 1)) & ~(PAIR - 1)
    start = jnp.sum(jnp.where(r_sub < row, padded, 0), axis=0, keepdims=True)
    tmp[...] = jnp.broadcast_to(row, (128, n_tiles)).T
    step = 128
    rank = jnp.zeros((1, n_tiles), jnp.int32)
    for i in range(0, n_tiles, step):
        t_sub = lax.broadcasted_iota(jnp.int32, (step, n_tiles), 0) + i
        earlier = (tmp[i : i + step, :1] == row) & (t_sub < t_lane)
        rank += jnp.sum(earlier.astype(jnp.int32), axis=0, keepdims=True)
    place = jnp.where(used, start + rank, -1)
    value = t_lane | (col_ref[...] << T_BITS) | (row << (T_BITS + C_BITS)) | (1 << 29)
    tmp[...] = jnp.broadcast_to(place, (128, n_tiles)).T
    places = tmp[:, :1]
    tmp[...] = jnp.broadcast_to(value, (128, n_tiles)).T
    values = tmp[:, :1]
    for j in range(0, length, 128):
        s_lane = lax.broadcasted_iota(jnp.int32, (n_tiles, 128), 1) + j
        got = jnp.sum(jnp.where(places == s_lane, values, 0), axis=0, keepdims=True)
        some = got > 0
        plan[0:1, j : j + 128] = got & ((1 << T_BITS) - 1)
        plan[1:2, j : j + 128] = jnp.where(
            some, (got >> T_BITS) & ((1 << C_BITS) - 1), zero_col
        )
        plan[2:3, j : j + 128] = jnp.where(
            some, (got >> (T_BITS + C_BITS)) & 511, n_rows
        )
    r_col = lax.broadcasted_iota(jnp.int32, (n_rows, 128), 0)
    piece = lax.broadcasted_iota(jnp.int32, (n_rows, 128), 1) * (n_rows // pieces)
    plan[3:4, 0:128] = jnp.sum(jnp.where(r_col < piece, padded, 0), axis=0, keepdims=True)


def fetch(parts, pieces, features, tile_row, tile_col, tile_count, recv_rows, recv_count, size):
    width, v_rows = features.shape
    slots = recv_rows.shape[2]
    n_tiles = tile_row.shape[1]
    n_rows = v_rows // size
    length = n_tiles + n_rows * (PAIR - 1) + GROUP
    length = -(-length // 128) * 128
    vm = pl.BlockSpec(memory_space=pltpu.VMEM)
    dma = pltpu.SemaphoreType.DMA
    return pl.pallas_call(
        functools.partial(fetch_kernel, parts, pieces, size),
        out_shape=(
            jax.ShapeDtypeStruct((width, parts * slots), jnp.bfloat16),
            jax.ShapeDtypeStruct((8, length), jnp.int32),
        ),
        in_specs=[
            vm, vm, pl.BlockSpec(memory_space=pltpu.SMEM), vm,
            pl.BlockSpec(memory_space=pltpu.SMEM),
            pl.BlockSpec(memory_space=pl.ANY),
        ],
        out_specs=(vm, vm),
        scratch_shapes=[
            pltpu.VMEM((width, v_rows), jnp.bfloat16),
            pltpu.VMEM((v_rows + 8, width), jnp.float32),
            pltpu.VMEM((parts, slots), jnp.int32),
            pltpu.VMEM((parts, slots), jnp.int32),
            pltpu.SMEM((parts, slots), jnp.int32),
            pltpu.VMEM((slots, width), jnp.float32),
            pltpu.VMEM((parts, width, slots), jnp.bfloat16),
            pltpu.VMEM((n_tiles, 128), jnp.int32),
            dma((1,)), dma((parts,)), dma((parts,)), dma((1,)), dma((parts,)), dma((parts,)),
        ],
        compiler_params=pltpu.CompilerParams(
            collective_id=0, has_side_effects=True, vmem_limit_bytes=VMEM
        ),
    )(tile_row, tile_col, tile_count, recv_rows, recv_count, features)


def piece_kernel(shift, pieces, plan, feat_hbm, remote_hbm, tiles, out, buf, rows, acc, sem, fsem):
    piece = lax.rem(lax.axis_index("feat") + shift, pieces)
    size = buf.shape[2]
    v_rows = feat_hbm.shape[1]
    r_rows = remote_hbm.shape[1]
    blocks = acc.shape[0] - 1
    first_row = piece * blocks
    first, last = plan[3, piece], plan[3, piece + 1]
    steps = (last - first + GROUP - 1) // GROUP

    load = pltpu.make_async_copy(feat_hbm, rows.at[:, pl.ds(0, v_rows)], fsem.at[0])
    load.start()
    load_remote = pltpu.make_async_copy(remote_hbm, rows.at[:, pl.ds(v_rows, r_rows)], fsem.at[1])
    load_remote.start()

    def issue(g):
        slot = lax.rem(g, BUFFERS)
        for u in range(GROUP):
            pltpu.make_async_copy(
                tiles.at[plan[0, first + g * GROUP + u]], buf.at[slot, u], sem.at[slot]
            ).start()

    for g in range(BUFFERS - 1):
        @pl.when(g < steps)
        def _():
            issue(g)

    rows[:, v_rows + r_rows :] = jnp.zeros((rows.shape[0], size), rows.dtype)
    acc[...] = jnp.zeros_like(acc)
    load.wait()
    load_remote.wait()

    def step(g, _):
        slot = lax.rem(g, BUFFERS)

        @pl.when(g + BUFFERS - 1 < steps)
        def _():
            issue(g + BUFFERS - 1)

        pltpu.make_async_copy(tiles.at[pl.ds(0, GROUP)], buf.at[slot], sem.at[slot]).wait()
        base = first + g * GROUP
        products = []
        for u in range(0, GROUP, PAIR):
            left = jnp.concatenate(
                [rows[:, lane_block(plan[1, base + u + k], size)] for k in range(PAIR)], axis=1
            )
            right = jnp.concatenate([buf[slot, u + k] for k in range(PAIR)], axis=1)
            products.append(
                lax.dot_general(
                    left, right, (((1,), (1,)), ((), ())), preferred_element_type=jnp.float32
                )
            )
        for u in range(0, GROUP, PAIR):
            r = plan[2, base + u] - first_row
            r = jnp.where((r < 0) | (r > blocks), blocks, r)
            acc[r] += products[u // PAIR]
        return 0

    lax.fori_loop(0, steps, step, 0)
    for i in range(blocks):
        out[:, i * size : (i + 1) * size] = acc[i].astype(out.dtype)


def one_piece(shift, pieces, plan, features, remote, tile_vals):
    width, v_rows = features.shape
    size = tile_vals.shape[1]
    own = v_rows // pieces
    whole = pl.BlockSpec(memory_space=pl.ANY)
    work = width * own * v_rows // 4
    return pl.pallas_call(
        functools.partial(piece_kernel, shift, pieces),
        out_shape=jax.ShapeDtypeStruct((width, own), jnp.bfloat16),
        in_specs=[pl.BlockSpec(memory_space=pltpu.SMEM), whole, whole, whole],
        out_specs=pl.BlockSpec(memory_space=pltpu.VMEM),
        scratch_shapes=[
            pltpu.VMEM((BUFFERS, GROUP, size, size), jnp.bfloat16),
            pltpu.VMEM((width, v_rows + remote.shape[1] + size), jnp.bfloat16),
            pltpu.VMEM((own // size + 1, width, size), jnp.float32),
            pltpu.SemaphoreType.DMA((BUFFERS,)),
            pltpu.SemaphoreType.DMA((2,)),
        ],
        compiler_params=pltpu.CompilerParams(vmem_limit_bytes=VMEM),
        cost_estimate=pl.CostEstimate(
            flops=work, bytes_accessed=tile_vals.size * 2 // pieces, transcendentals=0
        ),
    )(plan, features, remote, tile_vals)


def project_kernel(shifts, *refs):
    pieces = len(shifts)
    parts, (w, b, out) = refs[:pieces], refs[pieces:]
    z = lax.axis_index("feat")
    width = parts[0].shape[0]
    here = lane_block(pl.program_id(0), out.shape[0])
    left = jnp.concatenate([part[:, here] for part in parts], axis=0)
    right = jnp.concatenate(
        [w[pl.ds(pl.multiple_of(lax.rem(z - s + pieces, pieces) * width, width), width), :] for s in shifts],
        axis=0,
    )
    hidden = lax.dot_general(
        left, right, (((0,), (0,)), ((), ())), preferred_element_type=jnp.float32
    )
    out[...] = jnp.maximum(hidden + b[...], 0.0).astype(out.dtype)


def project(shifts, parts, weight, bias):
    width, own = parts[0].shape
    f_out = weight.shape[1]
    cut = own // 2
    return pl.pallas_call(
        functools.partial(project_kernel, shifts),
        grid=(own // cut,),
        out_shape=jax.ShapeDtypeStruct((own, f_out), jnp.bfloat16),
        in_specs=[pl.BlockSpec(memory_space=pltpu.VMEM)] * len(parts)
        + [
            pl.BlockSpec(weight.shape, lambda i: (0, 0)),
            pl.BlockSpec((1, f_out), lambda i: (0, 0)),
        ],
        out_specs=pl.BlockSpec((cut, f_out), lambda i: (i, 0)),
        compiler_params=pltpu.CompilerParams(vmem_limit_bytes=16 << 20),
    )(*parts, weight, bias.reshape(1, f_out))


def on_device(
    features, tile_vals, tile_row, tile_col, tile_count, recv_rows, recv_count, weight, bias
):
    parts = lax.axis_size("vert")
    pieces = lax.axis_size("feat")
    size = tile_vals.shape[1]
    remote, plan = fetch(
        parts, pieces, features, tile_row, tile_col, tile_count, recv_rows, recv_count, size
    )
    shifts = sorted(range(1, pieces), key=lambda s: -min(s, pieces - s)) + [0]
    got = []
    for s in shifts:
        piece = one_piece(s, pieces, plan, features, remote, tile_vals)
        if s:
            piece = lax.ppermute(piece, "feat", [(i, (i + s) % pieces) for i in range(pieces)])
        got.append(piece)
    return project(shifts, got, weight, bias)


def solution(mesh):
    in_specs = (
        P("feat", "vert"),
        P("vert", None, None),
        P("vert", None),
        P("vert", None),
        P("vert"),
        P("vert", None, None),
        P("vert", None),
        P(),
        P(),
    )
    out_specs = P(("vert", "feat"), None)
    return jax.shard_map(
        on_device, mesh=mesh, in_specs=in_specs, out_specs=out_specs, check_vma=False
    )
```
